32 devices in a mesh: groups: 2 (over x), wide: 16 (over z, y, core).
Axes of the slice: x: 2, y: 2, z: 4, core: 2. Of those that a mesh axis runs over, the one named last changes fastest.
Arguments:
- embeddings: bfloat16 [65536, 768], P(('groups', 'wide')), parts along dimension 0
- pca_basis: bfloat16 [768, 256], P('wide'), may hold values from -0.21875 to 0.21875
- pca_center: bfloat16 [768], P('wide'), may hold values from -6 to 6
- row_labels: int32 [65536], P(('groups', 'wide')), parts along dimension 0, may hold values from 0 to 63, as said below
- row_ranks: int32 [65536], P(('groups', 'wide')), parts along dimension 0, may hold values from 0 to 4095, as said below
Outputs:
- nearest: float32 [65536], P(('groups', 'wide')), parts along dimension 0
The draws below stay inside these ranges and needn't reach their ends.
There are 2 independent parts, one for each index of `groups`. The reference program is written for one: setup_inputs(seed, part) draws one part's arguments, and reference() takes and returns one part's arrays. A program takes and returns all parts, laid end to end along the dimension named above; an argument that names none is the same for every part. Nothing has to cross between parts.
Inputs may be any that keep to these rules, and one draw needn't show every extreme that they name: `row_labels`: clusters o * 4 to (o + 1) * 4 - 1 form owner group o. Each device's rows fall in every owner group with at most 256 rows; in every draw some owner groups get exactly 256 rows from every device. `row_ranks`: within each cluster the rows' ranks are 0 up to the cluster's size - 1, each once. A cluster holds at most 4096 rows, and in every draw some cluster holds exactly that many.
All inputs are finite; a program needn't handle non-finite values.
Results may differ from the reference program's by a relative error of at most 0.00053.
Values may be sent and summed in bfloat16 or wider, within the bound.
No kernel may reach another device: no remote copies, remote signals or barrier semaphores. Data moves between devices by JAX's collectives and lax.ppermute only.
A program may use at most 64 MiB of HBM per device.

```python
import jax
import jax.numpy as jnp
from jax import lax

D = 768
PC = 256
ROWS_DEV = 2048
CL_DEV = 4
ROWS = 32768
CLUSTERS = 64
SLOT = 256


def layout(key):
    peer_count = ROWS // ROWS_DEV
    quarter = peer_count // 4
    subkeys = jax.random.split(key, 7)
    ranking = jax.random.permutation(subkeys[0], peer_count)
    tier_level = jnp.where(ranking < quarter, 2, jnp.where(ranking < 2 * quarter, 1, 0))
    jitter = jax.random.randint(subkeys[1], (peer_count, peer_count), 0, 1 << 20)
    score = (jitter + tier_level[None, :] * (1 << 20)) * peer_count + jnp.arange(peer_count)[None, :]
    ranked = jnp.argsort(-score, axis=1)[:, :3 * quarter]
    shares = jax.random.randint(subkeys[2], (peer_count, quarter), 0, SLOT + 1)
    paired = jnp.stack([shares, SLOT - shares], axis=2).reshape(peer_count, 2 * quarter)
    counts = jnp.concatenate([jnp.full((peer_count, quarter), SLOT, jnp.int32), paired.astype(jnp.int32)], axis=1)
    bounds = jnp.cumsum(counts, axis=1)
    positions = jnp.arange(ROWS_DEV)
    owner_slot = jnp.sum((bounds[:, None, :] <= positions[None, :, None]).astype(jnp.int32), axis=2)
    owners = jnp.take_along_axis(ranked, owner_slot, axis=1)
    picked = jnp.minimum(jax.random.randint(subkeys[3], (peer_count, ROWS_DEV), 0, CL_DEV), jax.random.randint(subkeys[4], (peer_count, ROWS_DEV), 0, CL_DEV))
    picked = jnp.where(ranking[owners] == 0, 0, picked)
    labels_grid = owners * CL_DEV + picked
    mixing = jax.random.randint(subkeys[5], (peer_count, ROWS_DEV), 0, 4096) * ROWS_DEV + positions[None, :]
    labels = jnp.take_along_axis(labels_grid, jnp.argsort(mixing, axis=1), axis=1).reshape(-1).astype(jnp.int32)
    priority = jax.random.permutation(subkeys[6], ROWS)
    sort_order = jnp.argsort(labels * ROWS + priority)
    sorted_labels = labels[sort_order]
    starts = jnp.searchsorted(sorted_labels, sorted_labels, side='left')
    ranks = jnp.zeros((ROWS,), jnp.int32).at[sort_order].set((jnp.arange(ROWS) - starts).astype(jnp.int32))
    return (labels, ranks)


def draw_row_labels(key, part):
    return layout(key)[0]


def draw_row_ranks(key, part):
    return layout(key)[1]


def draw_embeddings(key, part):
    labels = layout(key)[0]
    key = jax.random.fold_in(key, 5)
    subkeys = jax.random.split(key, 2)
    centroids = jax.random.normal(subkeys[0], (CLUSTERS, D), jnp.float32)
    jitter = jax.random.normal(subkeys[1], (ROWS, D), jnp.float32)
    weight_mix = 0.8
    return (centroids[labels] * weight_mix + jitter).astype(jnp.bfloat16)


def shard_levels(stream_key, dims, shards, smallest, largest):
    def one(axis_at, shards_of):
        steps = jax.random.uniform(jax.random.fold_in(jax.random.fold_in(stream_key, 6), axis_at), (shards_of,), jnp.float32, smallest / len(shards), largest / len(shards))
        return jnp.repeat(jnp.exp(steps), dims[axis_at] // shards_of).reshape((-1,) + (1,) * (len(dims) - axis_at - 1))

    factor_of = one(*shards[0])
    for cut in shards[1:]:
        factor_of = factor_of * one(*cut)
    return factor_of


def normal_values(stream_key, dims, spread, bound, shards=(), kind=jnp.bfloat16):
    drawn = spread * jax.random.normal(stream_key, dims, jnp.float32)
    if shards:
        drawn = drawn * shard_levels(stream_key, dims, shards, -0.22, 0.18)
    return jnp.clip(drawn, -bound, bound).astype(kind)


def setup_inputs(seed: int = 0, part: int = 0) -> dict:
    streams_of = jax.random.split(jax.random.key(seed), 6)
    part_keys = jax.random.split(jax.random.fold_in(streams_of[5], part), 6)
    return {
        "embeddings": draw_embeddings(jax.random.fold_in(jax.random.fold_in(streams_of[5], part), 71), part),
        "pca_basis": normal_values(streams_of[1], (D, PC), D ** -0.5, 0.21875, ((0, 16),)),
        "pca_center": normal_values(streams_of[2], (D,), 1.0, 6.0, ((0, 16),)),
        "row_labels": draw_row_labels(jax.random.fold_in(jax.random.fold_in(streams_of[5], part), 71), part),
        "row_ranks": draw_row_ranks(jax.random.fold_in(jax.random.fold_in(streams_of[5], part), 71), part),
    }


def reference(embeddings, pca_basis, pca_center, row_labels, row_ranks):
    offset = jnp.dot(pca_center, pca_basis, preferred_element_type=jnp.float32)
    projected = jnp.dot(embeddings, pca_basis, preferred_element_type=jnp.float32) - offset[None, :]
    scale_back = lax.rsqrt(lax.optimization_barrier(jnp.sum(projected * projected, axis=1, keepdims=True)) + 1e-06)
    unit_rows = (projected * scale_back).astype(jnp.bfloat16)
    row_total = unit_rows.shape[0]
    block_rows = min(512, row_total)
    window_rows = 2 * ROWS_DEV
    sort_order = jnp.argsort(row_labels * row_total + row_ranks).astype(jnp.int32)
    sorted_units = unit_rows[sort_order]
    sorted_labels = row_labels[sort_order]
    padded_units = jnp.concatenate([jnp.zeros((window_rows, unit_rows.shape[1]), jnp.bfloat16), sorted_units], axis=0)
    padded_labels = jnp.concatenate([jnp.full((window_rows,), -1, jnp.int32), sorted_labels.astype(jnp.int32)], axis=0)

    def one_block(block_index):
        row_start = (block_index * block_rows).astype(jnp.int32)
        queries = lax.dynamic_slice_in_dim(sorted_units, row_start, block_rows, 0)
        query_labels = lax.dynamic_slice_in_dim(sorted_labels, row_start, block_rows, 0)
        columns = lax.dynamic_slice_in_dim(padded_units, row_start, window_rows + block_rows, 0)
        column_labels = lax.dynamic_slice_in_dim(padded_labels, row_start, window_rows + block_rows, 0)
        cosines = lax.dot_general(queries, columns, (((1,), (1,)), ((), ())), preferred_element_type=jnp.float32)
        query_places = row_start + jnp.arange(block_rows, dtype=jnp.int32)
        column_places = row_start - window_rows + jnp.arange(window_rows + block_rows, dtype=jnp.int32)
        allowed = (query_labels[:, None] == column_labels[None, :]) & (column_places[None, :] < query_places[:, None])
        return lax.optimization_barrier(jnp.max(jnp.where(allowed, cosines, jnp.float32(-1.0)), axis=1))
    sorted_best = lax.map(one_block, jnp.arange(row_total // block_rows, dtype=jnp.int32)).reshape(-1)
    return jnp.zeros((row_total,), jnp.float32).at[sort_order].set(sorted_best)
```

```python
import functools

import jax
import jax.numpy as jnp
from jax import lax
from jax.experimental import pallas as pl
from jax.experimental.pallas import tpu as pltpu
from jax.sharding import PartitionSpec as P

CL_DEV = 4
RANK_SPAN = 4096
KEY_LOW = 128
PIECE_TILE = 16
CHUNK = 256
IN_FLIGHT = 4
VMEM_BYTES = 48 * 1024 * 1024
VMEM = pl.BlockSpec(memory_space=pltpu.VMEM)
SMEM = pl.BlockSpec(memory_space=pltpu.SMEM)
F32 = jnp.float32
BF16 = jnp.bfloat16


def call(kernel, outs, operands, scratch=(), smem=(), flops=0, moved=0):
    return pl.pallas_call(
        kernel,
        out_shape=outs,
        in_specs=[SMEM if i in smem else VMEM for i in range(len(operands))],
        out_specs=jax.tree.map(lambda _: VMEM, outs),
        scratch_shapes=list(scratch),
        compiler_params=pltpu.CompilerParams(vmem_limit_bytes=VMEM_BYTES),
        cost_estimate=pl.CostEstimate(flops=flops, bytes_accessed=moved, transcendentals=0),
    )(*operands)


def masks_of(peers):
    far = list(range(peers // 2, peers))
    near = list(range(peers // 4, peers // 2)) + list(range(1, peers // 4))
    order = []
    for i in range(max(len(far), len(near))):
        order += far[i : i + 1] + near[i : i + 1]
    return order


def swap(x, mask, peers):
    return lax.ppermute(x, "wide", [(i, i ^ mask) for i in range(peers)])


def hits(owners, peers):
    return owners == lax.broadcasted_iota(jnp.int32, (peers, owners.shape[1]), 0)


def places_kernel(peers, slot, labels_ref, ranks_ref, place_ref, keys_ref):
    rows = labels_ref.shape[1]
    step = min(CHUNK, rows)
    labels = labels_ref[...]
    owners = labels // CL_DEV
    hit = hits(owners, peers)
    hit_f = jnp.where(hit, 1.0, 0.0)
    earlier = jnp.where(
        lax.broadcasted_iota(jnp.int32, (step, step), 0) < lax.broadcasted_iota(jnp.int32, (step, step), 1), 1.0, 0.0
    ).astype(BF16)
    seen = jnp.zeros((peers, 1), F32)
    within = []
    for b in range(rows // step):
        hit_b = hit_f[:, b * step : (b + 1) * step]
        counts = jnp.dot(hit_b.astype(BF16), earlier, preferred_element_type=F32) + seen
        within.append(jnp.sum(hit_b * counts, axis=0, keepdims=True))
        seen = seen + jnp.sum(hit_b, axis=1, keepdims=True)
    within = jnp.concatenate(within, axis=1).astype(jnp.int32)
    place_ref[...] = owners * slot + within
    keys = (labels % CL_DEV + 1) * RANK_SPAN + ranks_ref[...]
    high = (keys // KEY_LOW).astype(F32)
    low = (keys % KEY_LOW).astype(F32)
    spread = jnp.where(within == lax.broadcasted_iota(jnp.int32, (slot, rows), 0), 1.0, 0.0).astype(BF16)
    parts = jnp.concatenate([hit_f * high, hit_f * low], axis=0).astype(BF16)
    slots = lax.dot_general(parts, spread, (((1,), (1,)), ((), ())), preferred_element_type=F32)
    keys_ref[...] = (slots[:peers] * KEY_LOW + slots[peers:]).astype(jnp.int32)


def project(embeddings_ref, basis, offset, units_ref):
    rows = embeddings_ref.shape[0]
    step = min(CHUNK, rows)
    for b in range(rows // step):
        block = slice(b * step, (b + 1) * step)
        projected = jnp.dot(embeddings_ref[block], basis, preferred_element_type=F32) - offset
        scale_back = lax.rsqrt(jnp.sum(projected * projected, axis=1, keepdims=True) + 1e-06)
        units_ref[block] = (projected * scale_back).astype(BF16)


def project_whole_kernel(embeddings_ref, basis_ref, center_ref, units_ref):
    basis = basis_ref[...]
    offset = jnp.dot(center_ref[...], basis, preferred_element_type=F32)
    project(embeddings_ref, basis, offset, units_ref)


def project_pieces_kernel(spots, piece_rows, me_ref, embeddings_ref, gathered_ref, units_ref, basis_ref):
    tile = gathered_ref.shape[0] // len(spots)
    offset = None
    for q, mask in enumerate(spots):
        piece = gathered_ref[q * tile : q * tile + piece_rows]
        start = pl.multiple_of((me_ref[0] ^ mask) * piece_rows, piece_rows)
        basis_ref[pl.ds(start, piece_rows), :] = piece
        center = gathered_ref[q * tile + piece_rows : (q + 1) * tile, :piece_rows]
        part = jnp.dot(center, piece, preferred_element_type=F32)
        offset = part if offset is None else offset + part
    project(embeddings_ref, basis_ref[...], offset[:1], units_ref)


def slots_kernel(masks, me_ref, place_ref, units_ref, *out_refs):
    slot = out_refs[0].shape[0]
    rows = place_ref.shape[1]
    units = units_ref[...]
    for mask, out_ref in zip(masks, out_refs, strict=True):
        here = place_ref[...] - (me_ref[0] ^ mask) * slot
        spread = jnp.where(here == lax.broadcasted_iota(jnp.int32, (slot, rows), 0), 1.0, 0.0).astype(BF16)
        out_ref[...] = jnp.dot(spread, units, preferred_element_type=F32).astype(BF16)


def keys_kernel(masks, me_ref, keys_ref, row_ref, column_ref):
    slot = keys_ref.shape[1]
    for n, mask in enumerate(masks):
        keys = keys_ref[pl.ds(me_ref[0] ^ mask, 1), :]
        row_ref[:, n * slot : (n + 1) * slot] = keys
        column_ref[n * slot : (n + 1) * slot] = jnp.transpose(jnp.broadcast_to(keys, (128, slot)))


def pairs_kernel(starts, first, best_in_ref, row_ref, column_ref, *refs):
    *group_refs, best_ref, line_ref = refs
    new_ref = group_refs[-1]
    new_start = starts[len(group_refs) - 1]
    fresh = new_ref.shape[0]
    width = best_ref.shape[1]
    if first:
        best_ref[...] = jnp.full((1, width), -1.0, F32)
    else:
        best_ref[...] = best_in_ref[...]
    step = min(CHUNK, fresh)

    for t in range(fresh // step):
        rows = new_ref[t * step : (t + 1) * step]
        at = new_start + t * step
        key_col = column_ref[at : at + step]
        label_col = key_col // RANK_SPAN
        line_ref[...] = jnp.full(line_ref.shape, -1.0, F32)

        def pairs(others, lanes, both):
            cosines = lax.dot_general(rows, others, (((1,), (1,)), ((), ())), preferred_element_type=F32)
            for lane in range(0, others.shape[0], 128):
                key_row = row_ref[:, pl.ds(lanes + lane, 128)]
                label_row = key_row // RANK_SPAN
                down = None
                for s in range(0, step, 64):
                    c = cosines[s : s + 64, lane : lane + 128]
                    c = jnp.where(label_col[s : s + 64] == label_row, c, -1.0)
                    earlier = key_col[s : s + 64] < key_row
                    d = jnp.where(earlier, c, -1.0)
                    d = jnp.max(d.reshape(8, 8, 128), axis=0)
                    down = d if down is None else jnp.maximum(down, d)
                    if both:
                        line_ref[s : s + 64] = jnp.maximum(line_ref[s : s + 64], jnp.where(earlier, -1.0, c))
                here = pl.ds(lanes + lane, 128)
                best_ref[:, here] = jnp.maximum(best_ref[:, here], jnp.max(down, axis=0, keepdims=True))

        pairs(rows, at, False)
        for g, group_ref in enumerate(group_refs):
            count = t if g == len(group_refs) - 1 else group_ref.shape[0] // step
            if count:

                def one(i, carry, group_ref=group_ref, g=g):
                    start = pl.multiple_of(i * step, step)
                    pairs(group_ref[pl.ds(start, step), :], pl.multiple_of(starts[g] + start, 128), True)
                    return carry

                lax.fori_loop(0, count, one, 0)
        if t or len(group_refs) > 1:
            line = jnp.max(jnp.transpose(line_ref[...]), axis=0, keepdims=True)
            best_ref[:, at : at + step] = jnp.maximum(best_ref[:, at : at + step], line)


def back_kernel(masks, slot, place_ref, returned_ref, out_ref):
    peers = returned_ref.shape[0]
    place = place_ref[...]
    rows = place.shape[1]
    values = returned_ref[...]
    high = values.astype(BF16)
    rest = values - high.astype(F32)
    middle = rest.astype(BF16)
    low = (rest - middle.astype(F32)).astype(BF16)
    parts = jnp.concatenate([high, middle, low], axis=0)
    spread = jnp.where(place % slot == lax.broadcasted_iota(jnp.int32, (slot, rows), 0), 1.0, 0.0).astype(BF16)
    found = jnp.dot(parts, spread, preferred_element_type=F32)
    found = (found[:peers] + found[peers : 2 * peers]) + found[2 * peers :]
    out_ref[...] = jnp.sum(jnp.where(hits(place // slot, peers), found, 0.0), axis=0, keepdims=True)


def sds(shape, dtype):
    return jax.ShapeDtypeStruct(shape, dtype)


def shards(embeddings, pca_basis, pca_center, row_labels, row_ranks):
    peers = lax.axis_size("wide")
    me = lax.axis_index("wide").astype(jnp.int32).reshape(1)
    rows, depth = embeddings.shape
    width = pca_basis.shape[1]
    piece_rows = pca_basis.shape[0]
    slot = 2 * rows // peers
    order = masks_of(peers)
    masks = [0, *order]

    place, keys = call(
        functools.partial(places_kernel, peers, slot),
        (sds((1, rows), jnp.int32), sds((peers, slot), jnp.int32)),
        (row_labels.reshape(1, rows), row_ranks.reshape(1, rows)),
        flops=2 * 3 * peers * rows * slot,
    )
    got_keys = lax.all_to_all(keys, "wide", split_axis=0, concat_axis=0, tiled=True)

    cost = dict(flops=2 * rows * depth * width, moved=2 * rows * depth)
    if piece_rows % PIECE_TILE:
        basis = lax.all_gather(pca_basis, "wide", axis=0, tiled=True)
        center = lax.all_gather(pca_center, "wide", axis=0, tiled=True).reshape(1, depth)
        units = call(project_whole_kernel, sds((rows, width), BF16), (embeddings, basis, center), **cost)
    else:
        tail = jnp.zeros((PIECE_TILE, width), BF16).at[0, :piece_rows].set(pca_center)
        gathered = jnp.concatenate([pca_basis, tail], axis=0)
        spots = [0]
        bit = peers // 2
        while bit:
            gathered = jnp.concatenate([gathered, swap(gathered, bit, peers)], axis=0)
            spots = spots + [spot ^ bit for spot in spots]
            bit //= 2
        units = call(
            functools.partial(project_pieces_kernel, spots, piece_rows),
            sds((rows, width), BF16),
            (me, embeddings, gathered),
            scratch=[pltpu.VMEM((depth, width), BF16)],
            smem=(0,),
            **cost,
        )

    sent = []
    leading = min(IN_FLIGHT, len(order))
    for part in (order[:leading], order[leading:] + [0]):
        sent += call(
            functools.partial(slots_kernel, part),
            tuple(sds((slot, width), BF16) for _ in part),
            (me, place, units),
            smem=(0,),
            flops=2 * len(part) * slot * rows * width,
        )
    blocks = [sent[-1]]
    for n, mask in enumerate(order):
        block = sent[n]
        if n >= IN_FLIGHT:
            block, blocks[n - IN_FLIGHT + 1] = lax.optimization_barrier((block, blocks[n - IN_FLIGHT + 1]))
        blocks.append(swap(block, mask, peers))

    total = peers * slot
    key_row, key_column = call(
        functools.partial(keys_kernel, masks),
        (sds((1, total), jnp.int32), sds((total, 128), jnp.int32)),
        (me, got_keys),
        smem=(0,),
    )
    quarter, end = peers // 4, peers // 16
    cuts = [0, quarter, 2 * quarter, 3 * quarter, peers - end, peers]
    groups, starts = [], []
    best = jnp.zeros((1, total), F32)
    for lo, hi in zip(cuts[:-1], cuts[1:], strict=True):
        groups.append(jnp.concatenate(blocks[lo:hi], axis=0) if hi - lo > 1 else blocks[lo])
        starts.append(lo * slot)
        best = call(
            functools.partial(pairs_kernel, tuple(starts), lo == 0),
            sds((1, total), F32),
            (best, key_row, key_column, *groups),
            scratch=[pltpu.VMEM((min(CHUNK, (hi - lo) * slot), 128), F32)],
            flops=2 * (hi - lo) * slot * hi * slot * width,
        )
    best = best.reshape(peers, slot)
    source = jnp.bitwise_xor(me[0], jnp.asarray(masks, jnp.int32))
    best = jnp.zeros_like(best).at[source].set(best)
    returned = lax.all_to_all(best, "wide", split_axis=0, concat_axis=0, tiled=True)
    nearest = call(
        functools.partial(back_kernel, masks, slot),
        sds((1, rows), F32),
        (place, returned),
        flops=2 * 3 * peers * rows * slot,
    )
    return nearest.reshape(-1)


def solution(mesh):
    return jax.shard_map(
        shards,
        mesh=mesh,
        in_specs=(
            P(("groups", "wide"), None),
            P("wide", None),
            P("wide"),
            P(("groups", "wide")),
            P(("groups", "wide")),
        ),
        out_specs=P(("groups", "wide")),
        check_vma=False,
    )
```

```python
import functools

import jax
import jax.numpy as jnp
from jax import lax
from jax.experimental import pallas as pl
from jax.experimental.pallas import tpu as pltpu
from jax.sharding import PartitionSpec as P

CL_DEV = 4
RANK_SPAN = 4096
KEY_LOW = 128
PIECE_TILE = 16
CHUNK = 256
IN_FLIGHT = 4
VMEM_BYTES = 48 * 1024 * 1024
VMEM = pl.BlockSpec(memory_space=pltpu.VMEM)
SMEM = pl.BlockSpec(memory_space=pltpu.SMEM)
F32 = jnp.float32
BF16 = jnp.bfloat16


def call(kernel, outs, operands, scratch=(), smem=(), flops=0, moved=0):
    return pl.pallas_call(
        kernel,
        out_shape=outs,
        in_specs=[SMEM if i in smem else VMEM for i in range(len(operands))],
        out_specs=jax.tree.map(lambda _: VMEM, outs),
        scratch_shapes=list(scratch),
        compiler_params=pltpu.CompilerParams(vmem_limit_bytes=VMEM_BYTES),
        cost_estimate=pl.CostEstimate(flops=flops, bytes_accessed=moved, transcendentals=0),
    )(*operands)


def masks_of(peers):
    far = list(range(peers // 2, peers))
    near = list(range(peers // 4, peers // 2)) + list(range(1, peers // 4))
    order = []
    for i in range(max(len(far), len(near))):
        order += far[i : i + 1] + near[i : i + 1]
    return order


def swap(x, mask, peers):
    return lax.ppermute(x, "wide", [(i, i ^ mask) for i in range(peers)])


def hits(owners, peers):
    return owners == lax.broadcasted_iota(jnp.int32, (peers, owners.shape[1]), 0)


def places_kernel(peers, slot, labels_ref, ranks_ref, place_ref, keys_ref):
    rows = labels_ref.shape[1]
    step = min(CHUNK, rows)
    labels = labels_ref[...]
    owners = labels // CL_DEV
    hit = hits(owners, peers)
    hit_f = jnp.where(hit, 1.0, 0.0)
    earlier = jnp.where(
        lax.broadcasted_iota(jnp.int32, (step, step), 0) < lax.broadcasted_iota(jnp.int32, (step, step), 1), 1.0, 0.0
    ).astype(BF16)
    seen = jnp.zeros((peers, 1), F32)
    within = []
    for b in range(rows // step):
        hit_b = hit_f[:, b * step : (b + 1) * step]
        counts = jnp.dot(hit_b.astype(BF16), earlier, preferred_element_type=F32) + seen
        within.append(jnp.sum(hit_b * counts, axis=0, keepdims=True))
        seen = seen + jnp.sum(hit_b, axis=1, keepdims=True)
    within = jnp.concatenate(within, axis=1).astype(jnp.int32)
    place_ref[...] = owners * slot + within
    keys = (labels % CL_DEV + 1) * RANK_SPAN + ranks_ref[...]
    high = (keys // KEY_LOW).astype(F32)
    low = (keys % KEY_LOW).astype(F32)
    spread = jnp.where(within == lax.broadcasted_iota(jnp.int32, (slot, rows), 0), 1.0, 0.0).astype(BF16)
    parts = jnp.concatenate([hit_f * high, hit_f * low], axis=0).astype(BF16)
    slots = lax.dot_general(parts, spread, (((1,), (1,)), ((), ())), preferred_element_type=F32)
    keys_ref[...] = (slots[:peers] * KEY_LOW + slots[peers:]).astype(jnp.int32).reshape(peers, 1, slot)


def stage_kernel(embeddings_ref, staged_ref, semaphore):
    copy = pltpu.make_async_copy(embeddings_ref, staged_ref, semaphore)
    copy.start()
    copy.wait()


def project(embeddings_ref, basis, offset, units_ref):
    rows = embeddings_ref.shape[0]
    step = min(CHUNK, rows)
    for b in range(rows // step):
        block = slice(b * step, (b + 1) * step)
        projected = jnp.dot(embeddings_ref[block], basis, preferred_element_type=F32) - offset
        scale_back = lax.rsqrt(jnp.sum(projected * projected, axis=1, keepdims=True) + 1e-06)
        units_ref[block] = (projected * scale_back).astype(BF16)


def project_whole_kernel(embeddings_ref, basis_ref, center_ref, units_ref):
    basis = basis_ref[...]
    offset = jnp.dot(center_ref[...], basis, preferred_element_type=F32)
    project(embeddings_ref, basis, offset, units_ref)


def project_pieces_kernel(spots, piece_rows, me_ref, embeddings_ref, gathered_ref, units_ref, basis_ref):
    tile = gathered_ref.shape[0] // len(spots)
    offset = None
    for q, mask in enumerate(spots):
        piece = gathered_ref[q * tile : q * tile + piece_rows]
        start = pl.multiple_of((me_ref[0] ^ mask) * piece_rows, piece_rows)
        basis_ref[pl.ds(start, piece_rows), :] = piece
        center = gathered_ref[q * tile + piece_rows : (q + 1) * tile, :piece_rows]
        part = jnp.dot(center, piece, preferred_element_type=F32)
        offset = part if offset is None else offset + part
    project(embeddings_ref, basis_ref[...], offset[:1], units_ref)


def slots_kernel(masks, me_ref, place_ref, units_ref, *out_refs):
    slot = out_refs[0].shape[0]
    rows = place_ref.shape[1]
    units = units_ref[...]
    for mask, out_ref in zip(masks, out_refs, strict=True):
        here = place_ref[...] - (me_ref[0] ^ mask) * slot
        spread = jnp.where(here == lax.broadcasted_iota(jnp.int32, (slot, rows), 0), 1.0, 0.0).astype(BF16)
        out_ref[...] = jnp.dot(spread, units, preferred_element_type=F32).astype(BF16)


def keys_kernel(masks, me_ref, keys_ref, row_ref, column_ref):
    slot = keys_ref.shape[2]
    for n, mask in enumerate(masks):
        keys = keys_ref[me_ref[0] ^ mask]
        row_ref[:, n * slot : (n + 1) * slot] = keys
        column_ref[n * slot : (n + 1) * slot] = jnp.transpose(jnp.broadcast_to(keys, (128, slot)))


def best_of(cosine, key_col, label_col, key_row, label_row, below, beside):
    cosine = jnp.where(label_col == label_row, cosine, -1.0)
    earlier = key_col < key_row
    below = jnp.maximum(below, jnp.where(earlier, cosine, -1.0))
    if beside is not None:
        beside = jnp.maximum(beside, jnp.where(earlier, -1.0, cosine))
    return below, beside


def turned(line):
    return jnp.max(jnp.transpose(line), axis=0, keepdims=True)


def group_kernel(starts, last, *refs):
    olds = len(starts) - 1
    refs = list(refs)
    row_ref, column_ref = refs[:2]
    old_refs, new_ref = refs[2 : 2 + olds], refs[2 + olds]
    rest = refs[3 + olds :]
    best_in_ref = rest.pop(0) if olds else None
    line_in_ref = rest.pop(0) if olds > 1 else None
    best_ref = rest.pop(0)
    line_ref = rest.pop(0) if olds else None
    cosines_ref, turned_ref, all_ref = rest
    new_start, fresh = starts[-1], new_ref.shape[0]
    tiles = fresh // 128
    for t in range(0, fresh, 128):
        turned_ref[:, t : t + 128] = jnp.transpose(new_ref[t : t + 128].astype(F32)).astype(BF16)
    for start, old_ref in zip(starts[:-1], old_refs, strict=True):
        all_ref[start : start + old_ref.shape[0]] = old_ref[...]
    key_rows = [row_ref[:, new_start + t * 128 : new_start + (t + 1) * 128] for t in range(tiles)]
    label_rows = [key_row // RANK_SPAN for key_row in key_rows]

    def products(rows, buffer):
        cosines_ref[buffer, : rows.shape[0]] = jnp.dot(rows, turned_ref[...], preferred_element_type=F32)

    def maxima(at, step, line_from, buffer, below, keep):
        below = list(below)
        for s in range(0, step, 8):
            here = pl.ds(at + s, 8)
            key_col = column_ref[here, :]
            label_col = key_col // RANK_SPAN
            beside = None
            if keep:
                beside = jnp.full((8, 128), -1.0, F32) if line_from is None else line_from[here, :]
            for t in range(tiles):
                cosine = cosines_ref[buffer, s : s + 8, t * 128 : (t + 1) * 128]
                below[t], beside = best_of(
                    cosine, key_col, label_col, key_rows[t], label_rows[t], below[t], beside
                )
            if keep:
                line_ref[here, :] = beside
        return tuple(below)

    def sweep(rows_ref, lo, hi, shift, line_from, keep, below):
        step = CHUNK
        while (hi - lo) % (2 * step):
            step //= 2

        def two(i, below):
            at = pl.multiple_of(lo + i * 2 * step, step)
            products(rows_ref[pl.ds(at + step, step), :], 1)
            below = maxima(at + shift, step, line_from, 0, below, keep)
            after = pl.multiple_of(jnp.minimum(at + 2 * step, hi - step), step)
            products(rows_ref[pl.ds(after, step), :], 0)
            return maxima(at + step + shift, step, line_from, 1, below, keep)

        products(rows_ref[lo : lo + step], 0)
        return lax.fori_loop(0, (hi - lo) // (2 * step), two, below)

    below = tuple(jnp.full((8, 128), -1.0, F32) for _ in range(tiles))
    below = sweep(new_ref, 0, fresh, new_start, None, False, below)
    known = starts[-2] if olds > 1 else 0
    if known:
        below = sweep(all_ref, 0, known, 0, line_in_ref, True, below)
    if olds:
        below = sweep(all_ref, known, new_start, 0, None, True, below)
    best_ref[...] = jnp.full(best_ref.shape, -1.0, F32)
    if olds:
        best_ref[:, :new_start] = best_in_ref[:, :new_start]
    for t in range(tiles):
        here = slice(new_start + t * 128, new_start + (t + 1) * 128)
        best_ref[:, here] = jnp.max(below[t], axis=0, keepdims=True)
    if last:
        for at in range(0, new_start, 128):
            here = slice(at, at + 128)
            best_ref[:, here] = jnp.maximum(best_ref[:, here], turned(line_ref[here]))


def end_kernel(masks, starts, me_ref, best_in_ref, row_ref, column_ref, *refs):
    *old_refs, new_ref, best_ref, line_ref, all_ref = refs
    new_start, fresh = starts[-1], new_ref.shape[0]
    slot = best_ref.shape[2]
    new = new_ref[...]
    line_ref[...] = jnp.full(line_ref.shape, -1.0, F32)
    all_ref[...] = best_in_ref[...]
    for start, old_ref in zip(starts, [*old_refs, new_ref], strict=True):
        both = start < new_start
        for at in range(0, old_ref.shape[0], CHUNK):
            others = old_ref[at : at + CHUNK]
            cosines = lax.dot_general(new, others, (((1,), (1,)), ((), ())), preferred_element_type=F32)
            tiles = range(0, others.shape[0], 128)
            key_rows = [row_ref[:, start + at + t : start + at + t + 128] for t in tiles]
            label_rows = [key_row // RANK_SPAN for key_row in key_rows]
            below = [jnp.full((8, 128), -1.0, F32)] * len(tiles)
            for s in range(0, fresh, 8):
                key_col = column_ref[new_start + s : new_start + s + 8]
                label_col = key_col // RANK_SPAN
                beside = line_ref[s : s + 8] if both else None
                for n, t in enumerate(tiles):
                    below[n], beside = best_of(
                        cosines[s : s + 8, t : t + 128],
                        key_col, label_col, key_rows[n], label_rows[n], below[n], beside,
                    )
                if both:
                    line_ref[s : s + 8] = beside
            for n, t in enumerate(tiles):
                here = slice(start + at + t, start + at + t + 128)
                all_ref[:, here] = jnp.maximum(all_ref[:, here], jnp.max(below[n], axis=0, keepdims=True))
    for s in range(0, fresh, 128):
        here = slice(new_start + s, new_start + s + 128)
        all_ref[:, here] = jnp.maximum(all_ref[:, here], turned(line_ref[s : s + 128]))
    for n, mask in enumerate(masks):
        best_ref[me_ref[0] ^ mask] = all_ref[:, n * slot : (n + 1) * slot]


def back_kernel(slot, place_ref, returned_ref, out_ref):
    peers = returned_ref.shape[0]
    place = place_ref[...]
    rows = place.shape[1]
    values = returned_ref[...].reshape(peers, slot)
    high = values.astype(BF16)
    rest = values - high.astype(F32)
    middle = rest.astype(BF16)
    low = (rest - middle.astype(F32)).astype(BF16)
    parts = jnp.concatenate([high, middle, low], axis=0)
    spread = jnp.where(place % slot == lax.broadcasted_iota(jnp.int32, (slot, rows), 0), 1.0, 0.0).astype(BF16)
    found = jnp.dot(parts, spread, preferred_element_type=F32)
    found = (found[:peers] + found[peers : 2 * peers]) + found[2 * peers :]
    out_ref[...] = jnp.sum(jnp.where(hits(place // slot, peers), found, 0.0), axis=0, keepdims=True)


def sds(shape, dtype):
    return jax.ShapeDtypeStruct(shape, dtype)


def shards(embeddings, pca_basis, pca_center, row_labels, row_ranks):
    peers = lax.axis_size("wide")
    me = lax.axis_index("wide").astype(jnp.int32).reshape(1)
    rows, depth = embeddings.shape
    piece_rows, width = pca_basis.shape
    slot = 2 * rows // peers
    total = peers * slot
    order = masks_of(peers)
    masks = [0, *order]

    place, keys = call(
        functools.partial(places_kernel, peers, slot),
        (sds((1, rows), jnp.int32), sds((peers, 1, slot), jnp.int32)),
        (row_labels.reshape(1, rows), row_ranks.reshape(1, rows)),
        flops=2 * 3 * peers * rows * slot,
    )
    staged = pl.pallas_call(
        stage_kernel,
        out_shape=sds((rows, depth), BF16),
        in_specs=[pl.BlockSpec(memory_space=pl.ANY)],
        out_specs=VMEM,
        scratch_shapes=[pltpu.SemaphoreType.DMA],
        compiler_params=pltpu.CompilerParams(vmem_limit_bytes=VMEM_BYTES),
        cost_estimate=pl.CostEstimate(flops=0, bytes_accessed=4 * rows * depth, transcendentals=0),
    )(embeddings)

    cost = dict(flops=2 * rows * depth * width, moved=2 * rows * depth)
    if piece_rows % PIECE_TILE:
        basis = lax.all_gather(pca_basis, "wide", axis=0, tiled=True)
        center = lax.all_gather(pca_center, "wide", axis=0, tiled=True).reshape(1, depth)
        units = call(project_whole_kernel, sds((rows, width), BF16), (staged, basis, center), **cost)
    else:
        tail = jnp.pad(pca_center.reshape(1, piece_rows), ((0, PIECE_TILE - 1), (0, width - piece_rows)))
        gathered = lax.optimization_barrier(jnp.concatenate([pca_basis, tail], axis=0))
        spots = [0]
        bit = peers // 2
        beside = [(place, keys), (staged,)]
        while bit:
            gathered = jnp.concatenate([gathered, swap(gathered, bit, peers)], axis=0)
            if beside:
                gathered, *tied = lax.optimization_barrier((gathered, *beside.pop(0)))
                if len(tied) == 2:
                    place, keys = tied
                else:
                    (staged,) = tied
            spots = spots + [spot ^ bit for spot in spots]
            bit //= 2
        units = call(
            functools.partial(project_pieces_kernel, spots, piece_rows),
            sds((rows, width), BF16),
            (me, staged, gathered),
            scratch=[pltpu.VMEM((depth, width), BF16)],
            smem=(0,),
            **cost,
        )

    sent = []
    leading = min(IN_FLIGHT, len(order))
    for part in (order[:leading], order[leading:] + [0]):
        sent += call(
            functools.partial(slots_kernel, part),
            tuple(sds((slot, width), BF16) for _ in part),
            (me, place, units),
            smem=(0,),
            flops=2 * len(part) * slot * rows * width,
        )
    keys, sent[-1] = lax.optimization_barrier((keys, sent[-1]))
    got_keys = lax.all_to_all(keys, "wide", split_axis=0, concat_axis=0, tiled=True)
    blocks = [sent[-1]]
    for n, mask in enumerate(order):
        block = sent[n]
        if n >= IN_FLIGHT:
            block, blocks[n - IN_FLIGHT + 1] = lax.optimization_barrier((block, blocks[n - IN_FLIGHT + 1]))
        blocks.append(swap(block, mask, peers))

    key_row, key_column = call(
        functools.partial(keys_kernel, masks),
        (sds((1, total), jnp.int32), sds((total, 128), jnp.int32)),
        (me, got_keys),
        smem=(0,),
    )
    quarter, end = peers // 4, peers // 16
    cuts = [0, quarter, 2 * quarter, 3 * quarter, peers - end, peers]
    groups, starts, state = [], [], ()
    for lo, hi in zip(cuts[:-1], cuts[1:], strict=True):
        group = jnp.concatenate(blocks[lo:hi], axis=0) if hi - lo > 1 else blocks[lo]
        groups.append(group)
        starts.append(lo * slot)
        fresh = (hi - lo) * slot
        flops = 2 * fresh * hi * slot * width
        if hi < peers:
            state = call(
                functools.partial(group_kernel, tuple(starts), hi == peers - end),
                (sds((1, total), F32), *([sds((lo * slot, 128), F32)] if lo else [])),
                (key_row, key_column, *groups, *state),
                scratch=[
                    pltpu.VMEM((2, CHUNK, fresh), F32),
                    pltpu.VMEM((width, fresh), BF16),
                    pltpu.VMEM((max(lo * slot, 16), width), BF16),
                ],
                flops=flops,
            )
        else:
            best = call(
                functools.partial(end_kernel, masks, tuple(starts)),
                sds((peers, 1, slot), F32),
                (me, state[0], key_row, key_column, *groups),
                scratch=[pltpu.VMEM((fresh, 128), F32), pltpu.VMEM((1, total), F32)],
                smem=(0,),
                flops=flops,
            )
    returned = lax.all_to_all(best, "wide", split_axis=0, concat_axis=0, tiled=True)
    nearest = call(
        functools.partial(back_kernel, slot),
        sds((1, rows), F32),
        (place, returned),
        flops=2 * 3 * peers * rows * slot,
    )
    return nearest.reshape(-1)


def solution(mesh):
    return jax.shard_map(
        shards,
        mesh=mesh,
        in_specs=(
            P(("groups", "wide"), None),
            P("wide", None),
            P("wide"),
            P(("groups", "wide")),
            P(("groups", "wide")),
        ),
        out_specs=P(("groups", "wide")),
        check_vma=False,
    )
```

```python
import functools

import jax
import jax.numpy as jnp
from jax import lax
from jax.experimental import pallas as pl
from jax.experimental.pallas import tpu as pltpu
from jax.sharding import PartitionSpec as P

CL_DEV = 4
RANK_SPAN = 4096
KEY_LOW = 128
PIECE_TILE = 16
CHUNK = 256
LANES = 512
SLAB = 16
KEY_ROWS = 16
IN_FLIGHT = 5
VMEM_BYTES = 48 * 1024 * 1024
VMEM = pl.BlockSpec(memory_space=pltpu.VMEM)
SMEM = pl.BlockSpec(memory_space=pltpu.SMEM)
F32 = jnp.float32
BF16 = jnp.bfloat16


def call(kernel, outs, operands, scratch=(), smem=(), flops=0, moved=0):
    return pl.pallas_call(
        kernel,
        out_shape=outs,
        in_specs=[SMEM if i in smem else VMEM for i in range(len(operands))],
        out_specs=jax.tree.map(lambda _: VMEM, outs),
        scratch_shapes=list(scratch),
        compiler_params=pltpu.CompilerParams(vmem_limit_bytes=VMEM_BYTES),
        cost_estimate=pl.CostEstimate(flops=flops, bytes_accessed=moved, transcendentals=0),
    )(*operands)


def masks_of(peers):
    far = list(range(peers // 2, peers))
    near = list(range(peers // 4, peers // 2)) + list(range(1, peers // 4))
    order = []
    for i in range(len(near)):
        order += far[:-2][i : i + 1] + near[i : i + 1]
    return order + far[-2:]


def swap(x, mask, peers):
    return lax.ppermute(x, "wide", [(i, i ^ mask) for i in range(peers)])


def hits(owners, peers):
    return owners == lax.broadcasted_iota(jnp.int32, (peers, owners.shape[1]), 0)


def places_kernel(peers, slot, labels_ref, ranks_ref, place_ref, keys_ref):
    rows = labels_ref.shape[1]
    step = min(CHUNK, rows)
    labels = labels_ref[...]
    owners = labels // CL_DEV
    hit = hits(owners, peers)
    hit_f = jnp.where(hit, 1.0, 0.0)
    earlier = jnp.where(
        lax.broadcasted_iota(jnp.int32, (step, step), 0) < lax.broadcasted_iota(jnp.int32, (step, step), 1), 1.0, 0.0
    ).astype(BF16)
    seen = jnp.zeros((peers, 1), F32)
    within = []
    for b in range(rows // step):
        hit_b = hit_f[:, b * step : (b + 1) * step]
        counts = jnp.dot(hit_b.astype(BF16), earlier, preferred_element_type=F32) + seen
        within.append(jnp.sum(hit_b * counts, axis=0, keepdims=True))
        seen = seen + jnp.sum(hit_b, axis=1, keepdims=True)
    within = jnp.concatenate(within, axis=1).astype(jnp.int32)
    place_ref[...] = owners * slot + within
    keys = (labels % CL_DEV + 1) * RANK_SPAN + ranks_ref[...]
    high = (keys // KEY_LOW).astype(F32)
    low = (keys % KEY_LOW).astype(F32)
    spread = jnp.where(within == lax.broadcasted_iota(jnp.int32, (slot, rows), 0), 1.0, 0.0).astype(BF16)
    parts = jnp.concatenate([hit_f * high, hit_f * low], axis=0).astype(BF16)
    slots = lax.dot_general(parts, spread, (((1,), (1,)), ((), ())), preferred_element_type=F32)
    keys_ref[...] = (slots[:peers] * KEY_LOW + slots[peers:]).astype(jnp.int32).reshape(peers, 1, slot)


def stage_kernel(embeddings_ref, staged_ref, semaphore):
    copy = pltpu.make_async_copy(embeddings_ref, staged_ref, semaphore)
    copy.start()
    copy.wait()


def project(embeddings_ref, basis, offset, units_ref):
    rows = embeddings_ref.shape[0]
    step = min(CHUNK, rows)
    for b in range(rows // step):
        block = slice(b * step, (b + 1) * step)
        projected = jnp.dot(embeddings_ref[block], basis, preferred_element_type=F32) - offset
        scale_back = lax.rsqrt(jnp.sum(projected * projected, axis=1, keepdims=True) + 1e-06)
        units_ref[block] = (projected * scale_back).astype(BF16)


def fill_slots(masks, me_ref, place_ref, keys_ref, units_ref, out_refs):
    slot = keys_ref.shape[2]
    rows = place_ref.shape[1]
    units = units_ref[...]
    for mask, out_ref in zip(masks, out_refs, strict=True):
        owner = me_ref[0] ^ mask
        here = place_ref[...] - owner * slot
        spread = jnp.where(here == lax.broadcasted_iota(jnp.int32, (slot, rows), 0), 1.0, 0.0).astype(BF16)
        out_ref[:slot] = jnp.dot(spread, units, preferred_element_type=F32).astype(BF16)
        keys = keys_ref[owner]
        line = lax.broadcasted_iota(jnp.int32, (KEY_ROWS, slot), 0)
        parts = jnp.where(line == 0, keys // KEY_LOW, jnp.where(line == 1, keys % KEY_LOW, 0))
        out_ref[slot:, :slot] = parts.astype(F32).astype(BF16)


def slots_kernel(masks, me_ref, place_ref, keys_ref, units_ref, *out_refs):
    fill_slots(masks, me_ref, place_ref, keys_ref, units_ref, out_refs)


def project_whole_kernel(masks, me_ref, place_ref, keys_ref, embeddings_ref, basis_ref, center_ref, units_ref, *out_refs):
    basis = basis_ref[...]
    offset = jnp.dot(center_ref[...], basis, preferred_element_type=F32)
    project(embeddings_ref, basis, offset, units_ref)
    fill_slots(masks, me_ref, place_ref, keys_ref, units_ref, out_refs)


def project_pieces_kernel(masks, spots, piece_rows, me_ref, place_ref, keys_ref, embeddings_ref, *refs):
    *gathered_refs, units_ref = refs[: 3]
    out_refs, basis_ref = refs[3:-1], refs[-1]
    half = len(spots) // 2
    tile = gathered_refs[0].shape[0] // half
    offset = None
    for q, mask in enumerate(spots):
        gathered_ref, at = gathered_refs[q // half], q % half * tile
        piece = gathered_ref[at : at + piece_rows]
        start = pl.multiple_of((me_ref[0] ^ mask) * piece_rows, piece_rows)
        basis_ref[pl.ds(start, piece_rows), :] = piece
        center = gathered_ref[at + piece_rows : at + tile, :piece_rows]
        part = jnp.dot(center, piece, preferred_element_type=F32)
        offset = part if offset is None else offset + part
    project(embeddings_ref, basis_ref[...], offset[:1], units_ref)
    fill_slots(masks, me_ref, place_ref, keys_ref, units_ref, out_refs)


def best_of(cosine, key_col, label_col, key_row, label_row, below, beside):
    cosine = jnp.where(label_col == label_row, cosine, -1.0)
    earlier = key_col < key_row
    down = jnp.where(earlier, cosine, -1.0)
    down = jnp.max(down.reshape(-1, 8, 128), axis=0)
    below = jnp.maximum(below, down)
    if beside is not None:
        beside = jnp.maximum(beside, jnp.where(earlier, -1.0, cosine))
    return below, beside


def column_of(row):
    n = row.shape[1]
    same = lax.broadcasted_iota(jnp.int32, (n, n), 0) == lax.broadcasted_iota(jnp.int32, (n, n), 1)
    ones = jnp.ones((n, 128), BF16)
    parts = []
    for part in (row // KEY_LOW, row % KEY_LOW):
        spread = jnp.where(same, part.astype(F32), 0.0).astype(BF16)
        parts.append(jnp.dot(spread, ones, preferred_element_type=F32).astype(jnp.int32))
    return parts[0] * KEY_LOW + parts[1]


def pairs_kernel(fresh_blocks, masks, me_ref, *refs):
    refs = list(refs)
    state = (refs.pop(0), refs.pop(0)) if refs[0].shape[0] == 1 else None
    block_refs = refs[:-6]
    best_out_ref, row_out_ref, best_ref, line_ref, column_ref, all_ref = refs[-6:]
    width = all_ref.shape[1]
    slot = block_refs[0].shape[0] - KEY_ROWS
    start = (len(block_refs) - fresh_blocks) * slot
    fresh = fresh_blocks * slot
    end = start + fresh
    row_ref = row_out_ref
    best_ref[...] = jnp.full(best_ref.shape, -1.0, F32)
    if state is not None:
        row_ref[...] = state[1][...]
        best_ref[:, :start] = state[0][:, :start]
    else:
        row_ref[...] = jnp.zeros(row_ref.shape, jnp.int32)
    for n, block_ref in enumerate(block_refs):
        at = n * slot
        all_ref[at : at + slot] = block_ref[:slot]
        if at >= start:
            parts = block_ref[slot:].astype(F32)[:, :slot]
            row_ref[:, at : at + slot] = (parts[0:1] * KEY_LOW + parts[1:2]).astype(jnp.int32)
    step = min(CHUNK, fresh)
    for t in range(0, fresh, step):
        column_ref[t : t + step] = column_of(row_ref[:, start + t : start + t + step])
    line_ref[...] = jnp.full(line_ref.shape, -1.0, F32)

    def tile(t, lane, lanes, both):
        new = all_ref[start + t : start + t + step]
        others = all_ref[pl.ds(lane, lanes), :]
        cosines = lax.dot_general(new, others, (((1,), (1,)), ((), ())), preferred_element_type=F32)
        tiles = range(lanes // 128)
        heres = [pl.ds(lane + n * 128, 128) for n in tiles]
        key_rows = [row_ref[:, here] for here in heres]
        label_rows = [key_row // RANK_SPAN for key_row in key_rows]
        below = [jnp.full((8, 128), -1.0, F32)] * len(tiles)
        for s in range(0, step, SLAB):
            key_col = column_ref[t + s : t + s + SLAB]
            label_col = key_col // RANK_SPAN
            beside = line_ref[t + s : t + s + SLAB] if both else None
            for n in tiles:
                cosine = cosines[s : s + SLAB, n * 128 : (n + 1) * 128]
                below[n], beside = best_of(cosine, key_col, label_col, key_rows[n], label_rows[n], below[n], beside)
            if both:
                line_ref[t + s : t + s + SLAB] = beside
        for n, here in zip(tiles, heres, strict=True):
            best_ref[:, here] = jnp.maximum(best_ref[:, here], jnp.max(below[n], axis=0, keepdims=True))

    for t in range(0, fresh, step):
        tile(t, start + t, step, False)
        for lane in range(start, start + t, step):
            tile(t, lane, step, True)
    for lane in range(0, start, LANES):
        for t in range(0, fresh, step):
            tile(t, lane, min(LANES, start - lane), True)
    same = lax.broadcasted_iota(jnp.int32, (128, 128), 0) == lax.broadcasted_iota(jnp.int32, (128, 128), 1)
    for t in range(0, fresh, 128):
        here = slice(start + t, start + t + 128)
        column = jnp.max(line_ref[t : t + 128], axis=1, keepdims=True)
        turned = jnp.max(jnp.where(same, column, -1.0), axis=0, keepdims=True)
        best_ref[:, here] = jnp.maximum(best_ref[:, here], turned)
    if masks is None:
        best_out_ref[...] = best_ref[...]
    else:
        for n, mask in enumerate(masks):
            best_out_ref[me_ref[0] ^ mask] = best_ref[:, n * slot : (n + 1) * slot]


def back_kernel(slot, place_ref, returned_ref, out_ref):
    peers = returned_ref.shape[0]
    place = place_ref[...]
    rows = place.shape[1]
    values = returned_ref[...].reshape(peers, slot)
    high = values.astype(BF16)
    rest = values - high.astype(F32)
    middle = rest.astype(BF16)
    low = (rest - middle.astype(F32)).astype(BF16)
    parts = jnp.concatenate([high, middle, low], axis=0)
    spread = jnp.where(place % slot == lax.broadcasted_iota(jnp.int32, (slot, rows), 0), 1.0, 0.0).astype(BF16)
    found = jnp.dot(parts, spread, preferred_element_type=F32)
    found = (found[:peers] + found[peers : 2 * peers]) + found[2 * peers :]
    out_ref[...] = jnp.sum(jnp.where(hits(place // slot, peers), found, 0.0), axis=0, keepdims=True)


def sds(shape, dtype):
    return jax.ShapeDtypeStruct(shape, dtype)


def shards(embeddings, pca_basis, pca_center, row_labels, row_ranks):
    peers = lax.axis_size("wide")
    me = lax.axis_index("wide").astype(jnp.int32).reshape(1)
    rows, depth = embeddings.shape
    piece_rows, width = pca_basis.shape
    slot = 2 * rows // peers
    total = peers * slot
    order = masks_of(peers)
    masks = [0, *order]

    place, keys = call(
        functools.partial(places_kernel, peers, slot),
        (sds((1, rows), jnp.int32), sds((peers, 1, slot), jnp.int32)),
        (row_labels.reshape(1, rows), row_ranks.reshape(1, rows)),
        flops=2 * 3 * peers * rows * slot,
    )
    staged = pl.pallas_call(
        stage_kernel,
        out_shape=sds((rows, depth), BF16),
        in_specs=[pl.BlockSpec(memory_space=pl.ANY)],
        out_specs=VMEM,
        scratch_shapes=[pltpu.SemaphoreType.DMA],
        compiler_params=pltpu.CompilerParams(vmem_limit_bytes=VMEM_BYTES),
        cost_estimate=pl.CostEstimate(flops=0, bytes_accessed=4 * rows * depth, transcendentals=0),
    )(embeddings)

    leading = order[:1]
    followers = [order[1:3], order[3:IN_FLIGHT], [*order[IN_FLIGHT:], 0]]
    blocks_of = lambda part: tuple(sds((slot + KEY_ROWS, width), BF16) for _ in part)
    outs = (sds((rows, width), BF16), *blocks_of(leading))
    cost = dict(flops=2 * rows * width * (depth + len(leading) * slot), moved=2 * rows * depth)
    if piece_rows % PIECE_TILE:
        basis = lax.all_gather(pca_basis, "wide", axis=0, tiled=True)
        center = lax.all_gather(pca_center, "wide", axis=0, tiled=True).reshape(1, depth)
        kernel = functools.partial(project_whole_kernel, leading)
        units, *sent = call(kernel, outs, (me, place, keys, staged, basis, center), smem=(0,), **cost)
    else:
        tail = jnp.pad(pca_center.reshape(1, piece_rows), ((0, PIECE_TILE - 1), (0, width - piece_rows)))
        gathered = lax.optimization_barrier(jnp.concatenate([pca_basis, tail], axis=0))
        spots = [0]
        bit = peers // 2
        while bit:
            other = swap(gathered, bit, peers)
            spots = spots + [spot ^ bit for spot in spots]
            if len(spots) == 2:
                other, place, keys = lax.optimization_barrier((other, place, keys))
            elif len(spots) == 4:
                other, staged = lax.optimization_barrier((other, staged))
            if len(spots) < peers:
                gathered = lax.optimization_barrier(jnp.concatenate([gathered, other], axis=0))
            bit //= 2
        kernel = functools.partial(project_pieces_kernel, leading, spots, piece_rows)
        scratch = [pltpu.VMEM((depth, width), BF16)]
        operands = (me, place, keys, staged, gathered, other)
        units, *sent = call(kernel, outs, operands, scratch=scratch, smem=(0,), **cost)
    for part in followers:
        units, sent[-1] = lax.optimization_barrier((units, sent[-1]))
        sent += call(
            functools.partial(slots_kernel, part),
            blocks_of(part),
            (me, place, keys, units),
            smem=(0,),
            flops=2 * len(part) * slot * rows * width,
        )

    blocks = [sent[-1]]
    group, end = max(peers // 8, 1), max(peers // 16, 1)
    cuts = [*range(group, peers, group), peers - end, peers]
    state, done = (), 0

    def add_pairs(state, lo, hi):
        last = hi == peers
        fresh = (hi - lo) * slot
        return call(
            functools.partial(pairs_kernel, hi - lo, masks if last else None),
            (sds((peers, 1, slot) if last else (1, total), F32), sds((1, total), jnp.int32)),
            (me, *state, *blocks[:hi]),
            scratch=[
                pltpu.VMEM((1, total), F32),
                pltpu.VMEM((fresh, 128), F32),
                pltpu.VMEM((fresh, 128), jnp.int32),
                pltpu.VMEM((hi * slot, width), BF16),
            ],
            smem=(0,),
            flops=2 * fresh * hi * slot * width,
        )

    for n, mask in enumerate(order):
        block = sent[n]
        arrived = n + 1 - IN_FLIGHT
        if arrived > 0:
            while cuts[0] <= arrived + 1:
                state = add_pairs(state, done, cuts[0])
                done = cuts.pop(0)
            block, blocks[arrived], *state = lax.optimization_barrier((block, blocks[arrived], *state))
        blocks.append(swap(block, mask, peers))
    for cut in cuts:
        state = add_pairs(state, done, cut)
        done = cut
    best = state[0]
    returned = lax.all_to_all(best, "wide", split_axis=0, concat_axis=0, tiled=True)
    nearest = call(
        functools.partial(back_kernel, slot),
        sds((1, rows), F32),
        (place, returned),
        flops=2 * 3 * peers * rows * slot,
    )
    return nearest.reshape(-1)


def solution(mesh):
    return jax.shard_map(
        shards,
        mesh=mesh,
        in_specs=(
            P(("groups", "wide"), None),
            P("wide", None),
            P("wide"),
            P(("groups", "wide")),
            P(("groups", "wide")),
        ),
        out_specs=P(("groups", "wide")),
        check_vma=False,
    )
```

```python
import functools

import jax
import jax.numpy as jnp
from jax import lax
from jax.experimental import pallas as pl
from jax.experimental.pallas import tpu as pltpu
from jax.sharding import PartitionSpec as P

CL_DEV = 4
RANK_SPAN = 4096
KEY_LOW = 128
PIECE_TILE = 16
CHUNK = 256
LANES = 512
SLAB = 16
KEY_ROWS = 8
IN_FLIGHT = 4
VMEM_BYTES = 48 * 1024 * 1024
VMEM = pl.BlockSpec(memory_space=pltpu.VMEM)
SMEM = pl.BlockSpec(memory_space=pltpu.SMEM)
F32 = jnp.float32
BF16 = jnp.bfloat16


def call(kernel, outs, operands, scratch=(), smem=(), flops=0, moved=0):
    return pl.pallas_call(
        kernel,
        out_shape=outs,
        in_specs=[SMEM if i in smem else VMEM for i in range(len(operands))],
        out_specs=jax.tree.map(lambda _: VMEM, outs),
        scratch_shapes=list(scratch),
        compiler_params=pltpu.CompilerParams(vmem_limit_bytes=VMEM_BYTES),
        cost_estimate=pl.CostEstimate(flops=flops, bytes_accessed=moved, transcendentals=0),
    )(*operands)


def masks_of(peers):
    far = list(range(peers // 2, peers))
    near = list(range(1, peers // 2))
    order = []
    for i in range(len(far)):
        order += far[i : i + 1] + near[i : i + 1]
    return order


def swap(x, mask, peers):
    return lax.ppermute(x, "wide", [(i, i ^ mask) for i in range(peers)])


def hits(owners, peers):
    return owners == lax.broadcasted_iota(jnp.int32, (peers, owners.shape[1]), 0)


def places_kernel(peers, slot, labels_ref, ranks_ref, place_ref, keys_ref):
    rows = labels_ref.shape[1]
    step = min(CHUNK, rows)
    labels = labels_ref[...]
    owners = labels // CL_DEV
    hit = hits(owners, peers)
    hit_f = jnp.where(hit, 1.0, 0.0)
    earlier = jnp.where(
        lax.broadcasted_iota(jnp.int32, (step, step), 0) < lax.broadcasted_iota(jnp.int32, (step, step), 1), 1.0, 0.0
    ).astype(BF16)
    seen = jnp.zeros((peers, 1), F32)
    within = []
    for b in range(rows // step):
        hit_b = hit_f[:, b * step : (b + 1) * step]
        counts = jnp.dot(hit_b.astype(BF16), earlier, preferred_element_type=F32) + seen
        within.append(jnp.sum(hit_b * counts, axis=0, keepdims=True))
        seen = seen + jnp.sum(hit_b, axis=1, keepdims=True)
    within = jnp.concatenate(within, axis=1).astype(jnp.int32)
    place_ref[...] = owners * slot + within
    keys = (labels % CL_DEV + 1) * RANK_SPAN + ranks_ref[...]
    high = (keys // KEY_LOW).astype(F32)
    low = (keys % KEY_LOW).astype(F32)
    spread = jnp.where(within == lax.broadcasted_iota(jnp.int32, (slot, rows), 0), 1.0, 0.0).astype(BF16)
    parts = jnp.concatenate([hit_f * high, hit_f * low], axis=0).astype(BF16)
    slots = lax.dot_general(parts, spread, (((1,), (1,)), ((), ())), preferred_element_type=F32)
    keys_ref[...] = (slots[:peers] * KEY_LOW + slots[peers:]).astype(jnp.int32).reshape(peers, 1, slot)


def stage_kernel(embeddings_ref, staged_ref, semaphore):
    copy = pltpu.make_async_copy(embeddings_ref, staged_ref, semaphore)
    copy.start()
    copy.wait()


def project(embeddings_ref, basis, offset, units_ref):
    rows = embeddings_ref.shape[0]
    step = min(CHUNK, rows)
    for b in range(rows // step):
        block = slice(b * step, (b + 1) * step)
        projected = jnp.dot(embeddings_ref[block], basis, preferred_element_type=F32) - offset
        scale_back = lax.rsqrt(jnp.sum(projected * projected, axis=1, keepdims=True) + 1e-06)
        units_ref[block] = (projected * scale_back).astype(BF16)


def fill_slots(masks, me_ref, place_ref, keys_ref, units_ref, out_refs):
    slot = keys_ref.shape[2]
    rows = place_ref.shape[1]
    units = units_ref[...]
    for mask, out_ref in zip(masks, out_refs, strict=True):
        owner = me_ref[0] ^ mask
        here = place_ref[...] - owner * slot
        spread = jnp.where(here == lax.broadcasted_iota(jnp.int32, (slot, rows), 0), 1.0, 0.0).astype(BF16)
        out_ref[:slot] = jnp.dot(spread, units, preferred_element_type=F32).astype(BF16)
        keys = keys_ref[owner]
        line = lax.broadcasted_iota(jnp.int32, (KEY_ROWS, slot), 0)
        parts = jnp.where(line == 0, keys // KEY_LOW, jnp.where(line == 1, keys % KEY_LOW, 0))
        out_ref[slot:, :slot] = parts.astype(F32).astype(BF16)


def slots_kernel(masks, me_ref, place_ref, keys_ref, units_ref, *out_refs):
    fill_slots(masks, me_ref, place_ref, keys_ref, units_ref, out_refs)


def project_whole_kernel(masks, me_ref, place_ref, keys_ref, embeddings_ref, basis_ref, center_ref, units_ref, *out_refs):
    basis = basis_ref[...]
    offset = jnp.dot(center_ref[...], basis, preferred_element_type=F32)
    project(embeddings_ref, basis, offset, units_ref)
    fill_slots(masks, me_ref, place_ref, keys_ref, units_ref, out_refs)


def project_pieces_kernel(masks, spots, piece_rows, me_ref, place_ref, keys_ref, embeddings_ref, *refs):
    *gathered_refs, units_ref = refs[: 3]
    out_refs, basis_ref = refs[3:-1], refs[-1]
    half = len(spots) // 2
    tile = gathered_refs[0].shape[0] // half
    offset = None
    for q, mask in enumerate(spots):
        gathered_ref, at = gathered_refs[q // half], q % half * tile
        piece = gathered_ref[at : at + piece_rows]
        start = pl.multiple_of((me_ref[0] ^ mask) * piece_rows, piece_rows)
        basis_ref[pl.ds(start, piece_rows), :] = piece
        center = gathered_ref[at + piece_rows : at + tile, :piece_rows]
        part = jnp.dot(center, piece, preferred_element_type=F32)
        offset = part if offset is None else offset + part
    project(embeddings_ref, basis_ref[...], offset[:1], units_ref)
    fill_slots(masks, me_ref, place_ref, keys_ref, units_ref, out_refs)


def best_of(cosine, key_col, label_col, key_row, label_row, below, beside):
    cosine = jnp.where(label_col == label_row, cosine, -1.0)
    earlier = key_col < key_row
    down = jnp.where(earlier, cosine, -1.0)
    down = jnp.max(down.reshape(-1, 8, 128), axis=0)
    below = jnp.maximum(below, down)
    if beside is not None:
        beside = jnp.maximum(beside, jnp.where(earlier, -1.0, cosine))
    return below, beside


def column_of(row):
    n = row.shape[1]
    same = lax.broadcasted_iota(jnp.int32, (n, n), 0) == lax.broadcasted_iota(jnp.int32, (n, n), 1)
    ones = jnp.ones((n, 128), BF16)
    parts = []
    for part in (row // KEY_LOW, row % KEY_LOW):
        spread = jnp.where(same, part.astype(F32), 0.0).astype(BF16)
        parts.append(jnp.dot(spread, ones, preferred_element_type=F32).astype(jnp.int32))
    return parts[0] * KEY_LOW + parts[1]


def pairs_kernel(fresh_blocks, masks, me_ref, *refs):
    refs = list(refs)
    state = (refs.pop(0), refs.pop(0)) if refs[0].shape[0] == 1 else None
    block_refs = refs[:-6]
    best_out_ref, row_out_ref, best_ref, line_ref, column_ref, all_ref = refs[-6:]
    width = all_ref.shape[1]
    slot = block_refs[0].shape[0] - KEY_ROWS
    start = (len(block_refs) - fresh_blocks) * slot
    fresh = fresh_blocks * slot
    end = start + fresh
    row_ref = row_out_ref
    best_ref[...] = jnp.full(best_ref.shape, -1.0, F32)
    if state is not None:
        row_ref[...] = state[1][...]
        best_ref[:, :start] = state[0][:, :start]
    else:
        row_ref[...] = jnp.zeros(row_ref.shape, jnp.int32)
    for n, block_ref in enumerate(block_refs):
        at = n * slot
        all_ref[at : at + slot] = block_ref[:slot]
        if at >= start:
            parts = block_ref[slot:].astype(F32)[:, :slot]
            row_ref[:, at : at + slot] = (parts[0:1] * KEY_LOW + parts[1:2]).astype(jnp.int32)
    step = min(CHUNK, fresh)
    for t in range(0, fresh, step):
        column_ref[t : t + step] = column_of(row_ref[:, start + t : start + t + step])
    line_ref[...] = jnp.full(line_ref.shape, -1.0, F32)

    def tile(t, lane, lanes, both):
        new = all_ref[start + t : start + t + step]
        others = all_ref[pl.ds(lane, lanes), :]
        cosines = lax.dot_general(new, others, (((1,), (1,)), ((), ())), preferred_element_type=F32)
        tiles = range(lanes // 128)
        heres = [pl.ds(lane + n * 128, 128) for n in tiles]
        key_rows = [row_ref[:, here] for here in heres]
        label_rows = [key_row // RANK_SPAN for key_row in key_rows]
        below = [jnp.full((8, 128), -1.0, F32)] * len(tiles)
        for s in range(0, step, SLAB):
            key_col = column_ref[t + s : t + s + SLAB]
            label_col = key_col // RANK_SPAN
            beside = line_ref[t + s : t + s + SLAB] if both else None
            for n in tiles:
                cosine = cosines[s : s + SLAB, n * 128 : (n + 1) * 128]
                below[n], beside = best_of(cosine, key_col, label_col, key_rows[n], label_rows[n], below[n], beside)
            if both:
                line_ref[t + s : t + s + SLAB] = beside
        for n, here in zip(tiles, heres, strict=True):
            best_ref[:, here] = jnp.maximum(best_ref[:, here], jnp.max(below[n], axis=0, keepdims=True))

    for t in range(0, fresh, step):
        tile(t, start + t, step, False)
        for lane in range(start, start + t, step):
            tile(t, lane, step, True)
    for lane in range(0, start, LANES):
        for t in range(0, fresh, step):
            tile(t, lane, min(LANES, start - lane), True)
    same = lax.broadcasted_iota(jnp.int32, (128, 128), 0) == lax.broadcasted_iota(jnp.int32, (128, 128), 1)
    for t in range(0, fresh, 128):
        here = slice(start + t, start + t + 128)
        column = jnp.max(line_ref[t : t + 128], axis=1, keepdims=True)
        turned = jnp.max(jnp.where(same, column, -1.0), axis=0, keepdims=True)
        best_ref[:, here] = jnp.maximum(best_ref[:, here], turned)
    if masks is None:
        best_out_ref[...] = best_ref[...]
    else:
        for n, mask in enumerate(masks):
            best_out_ref[me_ref[0] ^ mask] = best_ref[:, n * slot : (n + 1) * slot]


def back_kernel(slot, place_ref, returned_ref, out_ref):
    peers = returned_ref.shape[0]
    place = place_ref[...]
    rows = place.shape[1]
    values = returned_ref[...].reshape(peers, slot)
    high = values.astype(BF16)
    rest = values - high.astype(F32)
    middle = rest.astype(BF16)
    low = (rest - middle.astype(F32)).astype(BF16)
    parts = jnp.concatenate([high, middle, low], axis=0)
    spread = jnp.where(place % slot == lax.broadcasted_iota(jnp.int32, (slot, rows), 0), 1.0, 0.0).astype(BF16)
    found = jnp.dot(parts, spread, preferred_element_type=F32)
    found = (found[:peers] + found[peers : 2 * peers]) + found[2 * peers :]
    out_ref[...] = jnp.sum(jnp.where(hits(place // slot, peers), found, 0.0), axis=0, keepdims=True)


def sds(shape, dtype):
    return jax.ShapeDtypeStruct(shape, dtype)


def shards(embeddings, pca_basis, pca_center, row_labels, row_ranks):
    peers = lax.axis_size("wide")
    me = lax.axis_index("wide").astype(jnp.int32).reshape(1)
    rows, depth = embeddings.shape
    piece_rows, width = pca_basis.shape
    slot = 2 * rows // peers
    total = peers * slot
    order = masks_of(peers)
    masks = [0, *order]

    place, keys = call(
        functools.partial(places_kernel, peers, slot),
        (sds((1, rows), jnp.int32), sds((peers, 1, slot), jnp.int32)),
        (row_labels.reshape(1, rows), row_ranks.reshape(1, rows)),
        flops=2 * 3 * peers * rows * slot,
    )
    staged = pl.pallas_call(
        stage_kernel,
        out_shape=sds((rows, depth), BF16),
        in_specs=[pl.BlockSpec(memory_space=pl.ANY)],
        out_specs=VMEM,
        scratch_shapes=[pltpu.SemaphoreType.DMA],
        compiler_params=pltpu.CompilerParams(vmem_limit_bytes=VMEM_BYTES),
        cost_estimate=pl.CostEstimate(flops=0, bytes_accessed=4 * rows * depth, transcendentals=0),
    )(embeddings)

    leading = order[:1]
    followers = [order[1:3], order[3:5], [*order[5:], 0]]
    blocks_of = lambda part: tuple(sds((slot + KEY_ROWS, width), BF16) for _ in part)
    outs = (sds((rows, width), BF16), *blocks_of(leading))
    cost = dict(flops=2 * rows * width * (depth + len(leading) * slot), moved=2 * rows * depth)
    if piece_rows % PIECE_TILE:
        basis = lax.all_gather(pca_basis, "wide", axis=0, tiled=True)
        center = lax.all_gather(pca_center, "wide", axis=0, tiled=True).reshape(1, depth)
        kernel = functools.partial(project_whole_kernel, leading)
        units, *sent = call(kernel, outs, (me, place, keys, staged, basis, center), smem=(0,), **cost)
    else:
        tail = jnp.pad(pca_center.reshape(1, piece_rows), ((0, PIECE_TILE - 1), (0, width - piece_rows)))
        gathered = lax.optimization_barrier(jnp.concatenate([pca_basis, tail], axis=0))
        spots = [0]
        bit = peers // 2
        while bit:
            other = swap(gathered, bit, peers)
            spots = spots + [spot ^ bit for spot in spots]
            if len(spots) == 2:
                other, place, keys = lax.optimization_barrier((other, place, keys))
            elif len(spots) == 4:
                other, staged = lax.optimization_barrier((other, staged))
            if len(spots) < peers:
                gathered = lax.optimization_barrier(jnp.concatenate([gathered, other], axis=0))
            bit //= 2
        kernel = functools.partial(project_pieces_kernel, leading, spots, piece_rows)
        scratch = [pltpu.VMEM((depth, width), BF16)]
        operands = (me, place, keys, staged, gathered, other)
        units, *sent = call(kernel, outs, operands, scratch=scratch, smem=(0,), **cost)
    for part in followers:
        units, sent[-1] = lax.optimization_barrier((units, sent[-1]))
        sent += call(
            functools.partial(slots_kernel, part),
            blocks_of(part),
            (me, place, keys, units),
            smem=(0,),
            flops=2 * len(part) * slot * rows * width,
        )

    blocks = [sent[-1]]
    step = max(peers // 16, 1)
    cuts = [*range(2 * step, peers, step), peers]
    state, done = (), 0

    def add_pairs(state, lo, hi):
        last = hi == peers
        fresh = (hi - lo) * slot
        return call(
            functools.partial(pairs_kernel, hi - lo, masks if last else None),
            (sds((peers, 1, slot) if last else (1, total), F32), sds((1, total), jnp.int32)),
            (me, *state, *blocks[:hi]),
            scratch=[
                pltpu.VMEM((1, total), F32),
                pltpu.VMEM((fresh, 128), F32),
                pltpu.VMEM((fresh, 128), jnp.int32),
                pltpu.VMEM((hi * slot, width), BF16),
            ],
            smem=(0,),
            flops=2 * fresh * hi * slot * width,
        )

    for n, mask in enumerate(order):
        block = sent[n]
        if n >= IN_FLIGHT:
            if cuts[0] <= n + 2 - IN_FLIGHT:
                state = add_pairs(state, done, cuts[0])
                done = cuts.pop(0)
            block, *state = lax.optimization_barrier((block, *state))
        blocks.append(swap(block, mask, peers))
    for cut in cuts:
        state = add_pairs(state, done, cut)
        done = cut
    best = state[0]
    returned = lax.all_to_all(best, "wide", split_axis=0, concat_axis=0, tiled=True)
    nearest = call(
        functools.partial(back_kernel, slot),
        sds((1, rows), F32),
        (place, returned),
        flops=2 * 3 * peers * rows * slot,
    )
    return nearest.reshape(-1)


def solution(mesh):
    return jax.shard_map(
        shards,
        mesh=mesh,
        in_specs=(
            P(("groups", "wide"), None),
            P("wide", None),
            P("wide"),
            P(("groups", "wide")),
            P(("groups", "wide")),
        ),
        out_specs=P(("groups", "wide")),
        check_vma=False,
    )
```

```python
import functools

import jax
import jax.numpy as jnp
from jax import lax
from jax.experimental import pallas as pl
from jax.experimental.pallas import tpu as pltpu
from jax.sharding import PartitionSpec as P

CL_DEV = 4
RANK_SPAN = 4096
KEY_LOW = 128
PIECE_TILE = 16
CHUNK = 256
LANES = 512
SLAB = 16
KEY_ROWS = 8
IN_FLIGHT = 4
LEADING = 3
FIRST = 5
VMEM_BYTES = 48 * 1024 * 1024
VMEM = pl.BlockSpec(memory_space=pltpu.VMEM)
SMEM = pl.BlockSpec(memory_space=pltpu.SMEM)
F32 = jnp.float32
BF16 = jnp.bfloat16


def call(kernel, outs, operands, scratch=(), smem=(), flops=0, moved=0):
    return pl.pallas_call(
        kernel,
        out_shape=outs,
        in_specs=[SMEM if i in smem else VMEM for i in range(len(operands))],
        out_specs=jax.tree.map(lambda _: VMEM, outs),
        scratch_shapes=list(scratch),
        compiler_params=pltpu.CompilerParams(vmem_limit_bytes=VMEM_BYTES),
        cost_estimate=pl.CostEstimate(flops=flops, bytes_accessed=moved, transcendentals=0),
    )(*operands)


def masks_of(peers):
    far = list(range(peers // 2, peers))
    near = list(range(1, peers // 2))
    order = []
    for i in range(len(far)):
        order += far[i : i + 1] + near[i : i + 1]
    return order


def swap(x, mask, peers):
    return lax.ppermute(x, "wide", [(i, i ^ mask) for i in range(peers)])


def hits(owners, peers):
    return owners == lax.broadcasted_iota(jnp.int32, (peers, owners.shape[1]), 0)


def places_kernel(peers, slot, labels_ref, ranks_ref, place_ref, keys_ref):
    rows = labels_ref.shape[1]
    step = min(CHUNK, rows)
    labels = labels_ref[...]
    owners = labels // CL_DEV
    hit = hits(owners, peers)
    hit_f = jnp.where(hit, 1.0, 0.0)
    earlier = jnp.where(
        lax.broadcasted_iota(jnp.int32, (step, step), 0) < lax.broadcasted_iota(jnp.int32, (step, step), 1), 1.0, 0.0
    ).astype(BF16)
    seen = jnp.zeros((peers, 1), F32)
    within = []
    for b in range(rows // step):
        hit_b = hit_f[:, b * step : (b + 1) * step]
        counts = jnp.dot(hit_b.astype(BF16), earlier, preferred_element_type=F32) + seen
        within.append(jnp.sum(hit_b * counts, axis=0, keepdims=True))
        seen = seen + jnp.sum(hit_b, axis=1, keepdims=True)
    within = jnp.concatenate(within, axis=1).astype(jnp.int32)
    place_ref[...] = owners * slot + within
    keys = (labels % CL_DEV + 1) * RANK_SPAN + ranks_ref[...]
    high = (keys // KEY_LOW).astype(F32)
    low = (keys % KEY_LOW).astype(F32)
    spread = jnp.where(within == lax.broadcasted_iota(jnp.int32, (slot, rows), 0), 1.0, 0.0).astype(BF16)
    parts = jnp.concatenate([hit_f * high, hit_f * low], axis=0).astype(BF16)
    slots = lax.dot_general(parts, spread, (((1,), (1,)), ((), ())), preferred_element_type=F32)
    keys_ref[...] = (slots[:peers] * KEY_LOW + slots[peers:]).astype(jnp.int32).reshape(peers, 1, slot)


def stage_kernel(embeddings_ref, staged_ref, semaphore):
    copy = pltpu.make_async_copy(embeddings_ref, staged_ref, semaphore)
    copy.start()
    copy.wait()


def spread_of(place_ref, owner, slot):
    here = place_ref[...] - owner * slot
    line = lax.broadcasted_iota(jnp.int32, (slot, place_ref.shape[1]), 0)
    return jnp.where(here == line, 1.0, 0.0).astype(BF16)


def lead_kernel(masks, slot, me_ref, place_ref, embeddings_ref, lead_ref):
    for n, mask in enumerate(masks):
        spread = spread_of(place_ref, me_ref[0] ^ mask, slot)
        rows = jnp.dot(spread, embeddings_ref[...], preferred_element_type=F32)
        lead_ref[n * slot : (n + 1) * slot] = rows.astype(BF16)


def project(rows, basis, offset):
    projected = jnp.dot(rows, basis, preferred_element_type=F32) - offset
    scale_back = lax.rsqrt(jnp.sum(projected * projected, axis=1, keepdims=True) + 1e-06)
    return (projected * scale_back).astype(BF16)


def fill_keys(owner, keys_ref, out_ref):
    slot = keys_ref.shape[2]
    keys = keys_ref[owner]
    line = lax.broadcasted_iota(jnp.int32, (KEY_ROWS, slot), 0)
    parts = jnp.where(line == 0, keys // KEY_LOW, jnp.where(line == 1, keys % KEY_LOW, 0))
    out_ref[slot:, :slot] = parts.astype(F32).astype(BF16)


def fill_lead(masks, me_ref, keys_ref, lead_ref, basis, offset, out_refs):
    slot = keys_ref.shape[2]
    for n, (mask, out_ref) in enumerate(zip(masks, out_refs, strict=True)):
        out_ref[:slot] = project(lead_ref[n * slot : (n + 1) * slot], basis, offset)
        fill_keys(me_ref[0] ^ mask, keys_ref, out_ref)


def first_whole_kernel(masks, me_ref, keys_ref, lead_ref, gathered_ref, center_ref, basis_ref, offset_ref, *out_refs):
    basis_ref[...] = gathered_ref[...]
    offset_ref[...] = jnp.dot(center_ref[...], basis_ref[...], preferred_element_type=F32)
    fill_lead(masks, me_ref, keys_ref, lead_ref, basis_ref[...], offset_ref[...], out_refs)


def first_pieces_kernel(masks, spots, piece_rows, me_ref, keys_ref, lead_ref, *refs):
    *gathered_refs, basis_ref, offset_ref = refs[:4]
    half = len(spots) // 2
    tile = gathered_refs[0].shape[0] // half
    offset = None
    for q, mask in enumerate(spots):
        gathered_ref, at = gathered_refs[q // half], q % half * tile
        piece = gathered_ref[at : at + piece_rows]
        start = pl.multiple_of((me_ref[0] ^ mask) * piece_rows, piece_rows)
        basis_ref[pl.ds(start, piece_rows), :] = piece
        center = gathered_ref[at + piece_rows : at + tile, :piece_rows]
        part = jnp.dot(center, piece, preferred_element_type=F32)
        offset = part if offset is None else offset + part
    offset_ref[...] = offset[:1]
    fill_lead(masks, me_ref, keys_ref, lead_ref, basis_ref[...], offset[:1], refs[4:])


def fill_slots(masks, me_ref, place_ref, keys_ref, units_ref, out_refs):
    slot = keys_ref.shape[2]
    units = units_ref[...]
    for mask, out_ref in zip(masks, out_refs, strict=True):
        owner = me_ref[0] ^ mask
        spread = spread_of(place_ref, owner, slot)
        out_ref[:slot] = jnp.dot(spread, units, preferred_element_type=F32).astype(BF16)
        fill_keys(owner, keys_ref, out_ref)


def units_kernel(masks, me_ref, place_ref, keys_ref, embeddings_ref, basis_ref, offset_ref, units_ref, *out_refs):
    rows = embeddings_ref.shape[0]
    step = min(CHUNK, rows)
    for b in range(0, rows, step):
        units_ref[b : b + step] = project(embeddings_ref[b : b + step], basis_ref[...], offset_ref[...])
    fill_slots(masks, me_ref, place_ref, keys_ref, units_ref, out_refs)


def slots_kernel(masks, me_ref, place_ref, keys_ref, units_ref, *out_refs):
    fill_slots(masks, me_ref, place_ref, keys_ref, units_ref, out_refs)


def best_of(cosine, key_col, label_col, key_row, label_row, below, beside):
    cosine = jnp.where(label_col == label_row, cosine, -1.0)
    earlier = key_col < key_row
    down = jnp.where(earlier, cosine, -1.0)
    down = jnp.max(down.reshape(-1, 8, 128), axis=0)
    below = jnp.maximum(below, down)
    if beside is not None:
        beside = jnp.maximum(beside, jnp.where(earlier, -1.0, cosine))
    return below, beside


def column_of(row):
    n = row.shape[1]
    same = lax.broadcasted_iota(jnp.int32, (n, n), 0) == lax.broadcasted_iota(jnp.int32, (n, n), 1)
    ones = jnp.ones((n, 128), BF16)
    parts = []
    for part in (row // KEY_LOW, row % KEY_LOW):
        spread = jnp.where(same, part.astype(F32), 0.0).astype(BF16)
        parts.append(jnp.dot(spread, ones, preferred_element_type=F32).astype(jnp.int32))
    return parts[0] * KEY_LOW + parts[1]


def pairs_kernel(fresh_blocks, masks, me_ref, *refs):
    refs = list(refs)
    best_in_ref = refs.pop(0) if refs[0].shape[0] == 1 else None
    *block_refs, best_out_ref, best_ref, line_ref, column_ref = refs
    slot = block_refs[0].shape[0] - KEY_ROWS
    start = (len(block_refs) - fresh_blocks) * slot
    fresh = fresh_blocks * slot
    step = min(CHUNK, fresh)
    if masks is None:
        best_ref = best_out_ref
    best_ref[:, start:] = jnp.full((1, best_ref.shape[1] - start), -1.0, F32)
    if start:
        best_ref[:, :start] = best_in_ref[:, :start]

    def units_of(at, count):
        pieces = [block_ref[:slot] for block_ref in block_refs[at // slot : (at + count) // slot]]
        return pieces[0] if len(pieces) == 1 else jnp.concatenate(pieces, axis=0)

    def keys_of(at, count):
        pieces = []
        for block_ref in block_refs[at // slot : (at + count) // slot]:
            parts = block_ref[slot:].astype(F32)[:, :slot]
            pieces.append((parts[0:1] * KEY_LOW + parts[1:2]).astype(jnp.int32))
        return pieces[0] if len(pieces) == 1 else jnp.concatenate(pieces, axis=1)

    for t in range(0, fresh, step):
        column_ref[t : t + step] = column_of(keys_of(start + t, step))

    def tile(t, lane, lanes, both):
        new, others = units_of(start + t, step), units_of(lane, lanes)
        cosines = lax.dot_general(new, others, (((1,), (1,)), ((), ())), preferred_element_type=F32)
        keys = keys_of(lane, lanes)
        tiles = range(lanes // 128)
        key_rows = [keys[:, n * 128 : (n + 1) * 128] for n in tiles]
        label_rows = [key_row // RANK_SPAN for key_row in key_rows]
        below = [jnp.full((8, 128), -1.0, F32)] * len(tiles)
        for s in range(0, step, SLAB):
            key_col = column_ref[t + s : t + s + SLAB]
            label_col = key_col // RANK_SPAN
            beside = None
            if both:
                beside = jnp.full((SLAB, 128), -1.0, F32) if fresh_line[t] else line_ref[t + s : t + s + SLAB]
            for n in tiles:
                cosine = cosines[s : s + SLAB, n * 128 : (n + 1) * 128]
                below[n], beside = best_of(cosine, key_col, label_col, key_rows[n], label_rows[n], below[n], beside)
            if both:
                line_ref[t + s : t + s + SLAB] = beside
        if both:
            fresh_line[t] = False
        for n in tiles:
            here = slice(lane + n * 128, lane + (n + 1) * 128)
            best_ref[:, here] = jnp.maximum(best_ref[:, here], jnp.max(below[n], axis=0, keepdims=True))

    fresh_line = {t: True for t in range(0, fresh, step)}
    for t in range(0, fresh, step):
        tile(t, start + t, step, False)
        for lane in range(start, start + t, step):
            tile(t, lane, step, True)
    for lane in range(0, start, LANES):
        for t in range(0, fresh, step):
            tile(t, lane, min(LANES, start - lane), True)
    same = lax.broadcasted_iota(jnp.int32, (128, 128), 0) == lax.broadcasted_iota(jnp.int32, (128, 128), 1)
    for t in range(0, fresh, 128):
        if not fresh_line[t // step * step]:
            here = slice(start + t, start + t + 128)
            column = jnp.max(line_ref[t : t + 128], axis=1, keepdims=True)
            turned = jnp.max(jnp.where(same, column, -1.0), axis=0, keepdims=True)
            best_ref[:, here] = jnp.maximum(best_ref[:, here], turned)
    if masks is not None:
        for n, mask in enumerate(masks):
            best_out_ref[me_ref[0] ^ mask] = best_ref[:, n * slot : (n + 1) * slot]


def back_kernel(slot, place_ref, returned_ref, out_ref):
    peers = returned_ref.shape[0]
    place = place_ref[...]
    rows = place.shape[1]
    values = returned_ref[...].reshape(peers, slot)
    high = values.astype(BF16)
    rest = values - high.astype(F32)
    middle = rest.astype(BF16)
    low = (rest - middle.astype(F32)).astype(BF16)
    parts = jnp.concatenate([high, middle, low], axis=0)
    spread = jnp.where(place % slot == lax.broadcasted_iota(jnp.int32, (slot, rows), 0), 1.0, 0.0).astype(BF16)
    found = jnp.dot(parts, spread, preferred_element_type=F32)
    found = (found[:peers] + found[peers : 2 * peers]) + found[2 * peers :]
    out_ref[...] = jnp.sum(jnp.where(hits(place // slot, peers), found, 0.0), axis=0, keepdims=True)


def sds(shape, dtype):
    return jax.ShapeDtypeStruct(shape, dtype)


def shards(embeddings, pca_basis, pca_center, row_labels, row_ranks):
    peers = lax.axis_size("wide")
    me = lax.axis_index("wide").astype(jnp.int32).reshape(1)
    rows, depth = embeddings.shape
    piece_rows, width = pca_basis.shape
    slot = 2 * rows // peers
    total = peers * slot
    order = masks_of(peers)
    masks = [0, *order]

    place, keys = call(
        functools.partial(places_kernel, peers, slot),
        (sds((1, rows), jnp.int32), sds((peers, 1, slot), jnp.int32)),
        (row_labels.reshape(1, rows), row_ranks.reshape(1, rows)),
        flops=2 * 3 * peers * rows * slot,
    )
    staged = pl.pallas_call(
        stage_kernel,
        out_shape=sds((rows, depth), BF16),
        in_specs=[pl.BlockSpec(memory_space=pl.ANY)],
        out_specs=VMEM,
        scratch_shapes=[pltpu.SemaphoreType.DMA],
        compiler_params=pltpu.CompilerParams(vmem_limit_bytes=VMEM_BYTES),
        cost_estimate=pl.CostEstimate(flops=0, bytes_accessed=4 * rows * depth, transcendentals=0),
    )(embeddings)

    first, second, third = order[:LEADING], order[LEADING:FIRST], [*order[FIRST:], 0]
    lead = call(
        functools.partial(lead_kernel, first, slot),
        sds((len(first) * slot, depth), BF16),
        (me, place, staged),
        smem=(0,),
    )

    blocks_of = lambda part: [sds((slot + KEY_ROWS, width), BF16) for _ in part]
    outs = [sds((depth, width), BF16), sds((1, width), F32), *blocks_of(first)]
    if piece_rows % PIECE_TILE:
        basis = lax.all_gather(pca_basis, "wide", axis=0, tiled=True)
        center = lax.all_gather(pca_center, "wide", axis=0, tiled=True).reshape(1, depth)
        kernel = functools.partial(first_whole_kernel, first)
        basis, offset, *sent = call(kernel, outs, (me, keys, lead, basis, center), smem=(0,))
    else:
        tail = jnp.pad(pca_center.reshape(1, piece_rows), ((0, KEY_ROWS - 1), (0, width - piece_rows)))
        gathered = lax.optimization_barrier(jnp.concatenate([pca_basis, tail], axis=0))
        spots = [0]
        bit = peers // 2
        while bit:
            other = swap(gathered, bit, peers)
            spots = spots + [spot ^ bit for spot in spots]
            if len(spots) == 2:
                other, place, keys = lax.optimization_barrier((other, place, keys))
            elif len(spots) == 4:
                other, staged = lax.optimization_barrier((other, staged))
            elif len(spots) == 8:
                other, lead = lax.optimization_barrier((other, lead))
            if len(spots) < peers:
                gathered = lax.optimization_barrier(jnp.concatenate([gathered, other], axis=0))
            bit //= 2
        kernel = functools.partial(first_pieces_kernel, first, spots, piece_rows)
        basis, offset, *sent = call(kernel, outs, (me, keys, lead, gathered, other), smem=(0,))
    ahead = swap(sent[1], order[1], peers)
    staged, ahead = lax.optimization_barrier((staged, ahead))
    units, *made = call(
        functools.partial(units_kernel, second),
        [sds((rows, width), BF16), *blocks_of(second)],
        (me, place, keys, staged, basis, offset),
        smem=(0,),
        flops=2 * rows * width * depth,
    )
    sent += made
    units, sent[-1] = lax.optimization_barrier((units, sent[-1]))
    sent += call(
        functools.partial(slots_kernel, third),
        blocks_of(third),
        (me, place, keys, units),
        smem=(0,),
        flops=2 * len(third) * slot * rows * width,
    )

    blocks = [sent[-1]]
    step = max(peers // 16, 1)
    cuts = [*range(2 * step, peers, step), peers]
    state, done = (), 0

    def add_pairs(state, lo, hi):
        last = hi == peers
        fresh = (hi - lo) * slot
        return call(
            functools.partial(pairs_kernel, hi - lo, masks if last else None),
            (sds((peers, 1, slot) if last else (1, total), F32),),
            (me, *state, *blocks[:hi]),
            scratch=[
                pltpu.VMEM((1, total), F32),
                pltpu.VMEM((fresh, 128), F32),
                pltpu.VMEM((fresh, 128), jnp.int32),
            ],
            smem=(0,),
            flops=2 * fresh * hi * slot * width,
        )

    for n, mask in enumerate(order):
        block = sent[n]
        if n >= FIRST:
            if cuts[0] <= n + 2 - IN_FLIGHT:
                state = add_pairs(state, done, cuts[0])
                done = cuts.pop(0)
            block, *state = lax.optimization_barrier((block, *state))
        blocks.append(ahead if n == 1 else swap(block, mask, peers))
    for cut in cuts:
        state = add_pairs(state, done, cut)
        done = cut
    best = state[0]
    returned = lax.all_to_all(best, "wide", split_axis=0, concat_axis=0, tiled=True)
    nearest = call(
        functools.partial(back_kernel, slot),
        sds((1, rows), F32),
        (place, returned),
        flops=2 * 3 * peers * rows * slot,
    )
    return nearest.reshape(-1)


def solution(mesh):
    return jax.shard_map(
        shards,
        mesh=mesh,
        in_specs=(
            P(("groups", "wide"), None),
            P("wide", None),
            P("wide"),
            P(("groups", "wide")),
            P(("groups", "wide")),
        ),
        out_specs=P(("groups", "wide")),
        check_vma=False,
    )
```
